256 devices in a mesh: tgt: 8 (over x, core), dp: 8 (over y, z_hi), vocab: 4 (over z_lo).
Axes of the slice: x: 4, y: 4, z: 8 (z_hi: 2, z_lo: 4; z = z_hi * 4 + z_lo), core: 2. Of those that a mesh axis runs over, the one named last changes fastest.
Arguments:
- hidden_rows: bfloat16 [3, 1024, 8192], P(None, 'dp', 'tgt'), may hold values from -384 to 384
- fc_weight: bfloat16 [3, 8192, 8192], P(None, 'tgt', ('dp', 'vocab')), may hold values from -0.0390625 to 0.0390625
- head_weight: bfloat16 [8192, 16384], P(('dp', 'vocab'), 'tgt'), may hold values from -0.0625 to 0.0625
- target_probs: bfloat16 [1024, 16384], P('dp', ('tgt', 'vocab')), may hold values from 0 to 1, as said below
- token_ids: int32 [1024], replicated, may hold values from 0 to 128255
- vocab_map: int32 [128256], replicated, may hold values from 0 to 16383
- segment_ids: int32 [1024], replicated, may hold values from 0 to 3, never falling along the last dimension, each value on 1 to 512 neighbouring positions
- loss_mask: int32 [1024], replicated, may hold values 0 or 1
Outputs:
- fc_step: float32 [3, 8192, 8192], P(None, 'tgt', ('dp', 'vocab'))
- head_step: float32 [8192, 16384], P(('dp', 'vocab'), 'tgt')
- loss: float32 [], replicated
The draws below stay inside these ranges and needn't reach their ends.
Inputs may be any that keep to these rules, and one draw needn't show every extreme that they name: `target_probs`: each row is a probability distribution over the 16384 draft tokens.
All inputs are finite; a program needn't handle non-finite values.
Results may differ from the reference program's by a relative error of at most 0.006.
Values may be sent and summed in bfloat16 or wider, within the bound.
No kernel may reach another device: no remote copies, remote signals or barrier semaphores. Data moves between devices by JAX's collectives and lax.ppermute only.
A program may use at most 128 MiB of HBM per device.

```python
import math
import jax
import jax.numpy as jnp
import numpy as np
from jax import lax

D = 8192
VT = 128256
VD = 16384
TOKENS = 1024


def draw_hidden_rows(key, part):
    key = jax.random.fold_in(key, 11)
    first_key = jax.random.fold_in(key, 0)
    values = jnp.clip(jax.random.normal(first_key, (3, TOKENS, D), jnp.float32), -6.0, 6.0)
    return values.astype(jnp.bfloat16)


def spread_rows(values, sharpness, fall):
    scaled = values * sharpness
    position = jnp.arange(VD, dtype=jnp.float32)[None, :] / VD
    weights = jnp.exp(scaled - jnp.max(scaled, axis=1, keepdims=True)) * jnp.exp(-math.log(fall) * position)
    return weights / jnp.sum(weights, axis=1, keepdims=True)


def draw_target_probs(key, part):
    key = jax.random.fold_in(key, 23)
    first_key, second_key = jax.random.split(key)
    sharpness = jnp.exp(jax.random.uniform(second_key, (TOKENS, 1), jnp.float32, math.log(0.5), math.log(3.0)))
    values = jax.random.normal(first_key, (TOKENS, VD), jnp.float32)
    probs = spread_rows(values, sharpness, 10.0)
    return probs.astype(jnp.bfloat16)


def place_ends(values, key, least, high):
    spot = [jax.random.randint(jax.random.fold_in(key, axis), (), 0, length) for axis, length in enumerate(values.shape)]
    longest = values.shape.index(max(values.shape))
    neighbour = spot[:longest] + [(spot[longest] + 1) % values.shape[longest]] + spot[longest + 1:]
    return values.at[tuple(spot)].set(least).at[tuple(neighbour)].set(high)


def block_scale(stream_key, extent, cuts, least, top_value):
    gain = 1.0
    for axis_at, parts in cuts:
        heights = jax.random.uniform(jax.random.fold_in(jax.random.fold_in(stream_key, 6), axis_at), (parts,), jnp.float32, least / len(cuts), top_value / len(cuts))
        gain = gain * jnp.repeat(jnp.exp(heights), extent[axis_at] // parts).reshape((-1,) + (1,) * (len(extent) - 1 - axis_at))
    return gain


def ranked_wide(own_key, shape, amount, lean):
    weights = [min(1 << octave, amount + 1 - (1 << octave)) * (1 << 20) // math.isqrt((1 << octave) ** lean) + 1 for octave in range((amount + 1).bit_length()) if 1 << octave <= amount]
    spread = 1 + sum(weights) // (1 << 30)
    listing = np.cumsum(np.array([max(1, weight // spread) for weight in weights]))
    ticket = jax.random.randint(jax.random.fold_in(own_key, 1), shape, 0, int(listing[len(weights) - 1]))
    start = jnp.left_shift(1, jnp.searchsorted(jnp.asarray(listing, jnp.int32), ticket, side="right").astype(jnp.int32))
    standing = start - 1 + jax.random.randint(jax.random.fold_in(own_key, 4), shape, 0, 1 << 30) % jnp.minimum(start, amount + 1 - start)
    return jax.random.permutation(jax.random.fold_in(own_key, 2), amount)[standing].astype(jnp.int32)


def profile(number_of, total, most, skew):
    loads = [(1 << 20) // math.isqrt(grade ** skew) + 1 for grade in range(2, number_of + 1)]
    rest, given = total - most - (number_of - 1), [1] * (number_of - 1)
    while rest > 0:
        candidates = [i for i in range(number_of - 1) if given[i] < most]
        pool, budget = sum([loads[i] for i in candidates]), rest
        for i in candidates:
            addition = min(most - given[i], max(1, budget * loads[i] // pool), rest)
            given[i] = given[i] + addition
            rest = rest - addition
    return np.array([most] + given)


def ragged(key, count, total, reach, slope):
    if count == 2:
        one = jax.random.randint(key, (), max(1, total - reach), min(reach, total - 1) + 1)
        return jnp.stack([one, total - one])
    sizes = jnp.asarray(profile(count, total, reach, slope), jnp.int32)
    couples = (count - 1) // 2
    donor, sink = sizes[1:1 + 2 * couples:2], sizes[2:2 + 2 * couples:2]
    margin = jnp.minimum(donor - 1, reach - sink)
    passed = jax.random.randint(jax.random.fold_in(key, 1), (couples,), 0, 1 << 20) % (margin + 1)
    sizes = sizes.at[1:1 + 2 * couples:2].set(donor - passed).at[2:2 + 2 * couples:2].set(sink + passed)
    return sizes[jax.random.permutation(jax.random.fold_in(key, 2), count)]


def bell_draw(stream_key, dims, scale, reach, pieces=(), kind=jnp.bfloat16):
    values = jax.random.normal(stream_key, dims, jnp.float32) * scale
    if len(pieces) > 0:
        values = block_scale(stream_key, dims, pieces, -0.22, 0.18) * values
    return jnp.clip(values, min=-reach, max=reach).astype(kind)


def setup_inputs(seed: int = 0) -> dict:
    splits = jax.random.split(jax.random.key(seed), 9)
    hidden_rows = draw_hidden_rows(jax.random.fold_in(splits[8], 71), 0)
    fc_weight = bell_draw(splits[1], (3, D, D), (3 * D) ** -0.5, 0.0390625, ((1, 8), (2, 32)))
    head_weight = bell_draw(splits[2], (D, VD), D ** -0.5, 0.0625, ((0, 32), (1, 8)))
    target_probs = draw_target_probs(jax.random.fold_in(splits[8], 71), 0)
    token_ids = place_ends(ranked_wide(splits[4], (TOKENS,), VT, 2), jax.random.fold_in(splits[4], 3), 0, VT - 1).astype(jnp.int32)
    vocab_map = place_ends(jax.random.randint(splits[5], (VT,), 0, VD), jax.random.fold_in(splits[5], 1), 0, VD - 1).astype(jnp.int32)
    segment_ids = jnp.searchsorted(jnp.cumsum(ragged(splits[6], 4, TOKENS, TOKENS // 2, 1)), jnp.arange(TOKENS), side="right").astype(jnp.int32)
    loss_mask = place_ends((jax.random.randint(splits[7], (TOKENS,), 0, 4) < 3).astype(jnp.int32), jax.random.fold_in(splits[7], 1), 0, 1)
    return dict(hidden_rows=hidden_rows, fc_weight=fc_weight, head_weight=head_weight, target_probs=target_probs, token_ids=token_ids, vocab_map=vocab_map, segment_ids=segment_ids, loss_mask=loss_mask)


def reference(hidden_rows, fc_weight, head_weight, target_probs, token_ids, vocab_map, segment_ids, loss_mask):
    highest = lax.Precision.HIGHEST
    rows_wide = hidden_rows.astype(jnp.float32)
    joined_acc = jnp.zeros((TOKENS, D), jnp.float32)
    for which in range(3):
        joined_acc = joined_acc + jnp.dot(rows_wide[which], fc_weight[which].astype(jnp.float32), precision=highest)
    joined_rows = joined_acc.astype(jnp.bfloat16)
    head_wide = head_weight.astype(jnp.float32)
    logits = jnp.dot(joined_rows.astype(jnp.float32), head_wide, precision=highest)
    row_peak = lax.optimization_barrier(jnp.max(logits, axis=1))
    exp_total = lax.optimization_barrier(jnp.sum(jnp.exp(logits - row_peak[:, None]), axis=1))
    log_total = row_peak + jnp.log(exp_total)
    draft_probs = jnp.exp(logits - log_total[:, None])
    labels = vocab_map[token_ids].astype(jnp.int32)
    picked = jnp.take_along_axis(logits, labels[:, None], axis=1)[:, 0]
    targets = target_probs.astype(jnp.float32)
    dotted = lax.optimization_barrier(jnp.sum(targets * logits, axis=1))
    prob_mass = lax.optimization_barrier(jnp.sum(targets, axis=1))
    next_segment = jnp.concatenate([segment_ids[1:], jnp.full((1,), -1, jnp.int32)])
    kept_tokens = loss_mask * (segment_ids == next_segment).astype(jnp.int32)
    kept_count = jnp.maximum(jnp.sum(kept_tokens), 1).astype(jnp.float32)
    kept_float = kept_tokens.astype(jnp.float32)
    token_loss = kept_float * (log_total * prob_mass - dotted + log_total - picked)
    loss = jnp.sum(token_loss) / kept_count
    onehot = (labels[:, None] == jnp.arange(VD, dtype=jnp.int32)[None, :]).astype(jnp.float32)
    dlogits = (kept_float[:, None] * (draft_probs * (prob_mass[:, None] + 1.0) - targets - onehot)).astype(jnp.bfloat16)
    dlogits_wide = dlogits.astype(jnp.float32)
    head_grad = jnp.dot(joined_rows.astype(jnp.float32).T, dlogits_wide, precision=highest)
    feature_grad = jnp.dot(dlogits_wide, head_wide.T, precision=highest).astype(jnp.bfloat16)
    feature_wide = feature_grad.astype(jnp.float32)
    fc_grad = jnp.stack([jnp.dot(rows_wide[which].T, feature_wide, precision=highest) for which in range(3)])
    squares = jnp.sum(head_grad * head_grad) + jnp.sum(fc_grad * fc_grad)
    entries = 3.0 * D * D + 1.0 * D * VD
    scale = lax.rsqrt(squares / entries + 1e-06)
    return (fc_grad * scale, head_grad * scale, loss)
```

```python
import jax
import jax.numpy as jnp
from jax import lax
from jax.sharding import Mesh, PartitionSpec as P

D = 8192
VD = 16384
X, C, Y, ZH, ZL = 4, 2, 4, 2, 4
Z = ZH * ZL
DEPTH = ("zh", "zl")


def spread(value, axes, count):
    return lax.all_to_all(jnp.broadcast_to(value[None], (count,) + value.shape), axes, 0, 0)


def swap(value):
    return lax.ppermute(value, "core", [(0, 1), (1, 0)])


def both_cores(value):
    other = swap(value)
    first = lax.axis_index("core") == 0
    return jnp.stack([jnp.where(first, value, other), jnp.where(first, other, value)])


def pick(value, index, axis):
    return lax.dynamic_index_in_dim(value, index, axis, keepdims=False)


def per_device(
    hidden_rows, fc_weight, head_weight, target_probs, token_ids, vocab_map, segment_ids, loss_mask
):
    x, core, y = lax.axis_index("x"), lax.axis_index("core"), lax.axis_index("y")
    zh, zl = lax.axis_index("zh"), lax.axis_index("zl")
    rows = hidden_rows.shape[1]
    quarter = rows // ZL
    tokens = rows * Y * ZH
    low = tokens // (Y * ZH * X)
    width = fc_weight.shape[2]
    depth = width * Z
    slab = head_weight.shape[1] // Z
    columns = slab * X

    piece = lax.dynamic_slice_in_dim(hidden_rows, zl * quarter, quarter, 1)
    piece = piece.transpose(1, 0, 2).reshape(quarter, -1)
    gathered = lax.all_gather(piece, ("y", "zh", "zl"), axis=0, tiled=True)
    fc_flat = fc_weight.reshape(-1, width)

    head = head_weight.reshape(width, ZL, ZH, slab).transpose(2, 1, 0, 3).reshape(Z, width, slab)
    head = lax.all_to_all(head, DEPTH, 0, 0).reshape(depth, slab)
    head = lax.all_gather(head, "x", axis=1, tiled=True)

    targets = target_probs.reshape(X, low, ZH, slab).transpose(0, 2, 1, 3)
    targets = targets.reshape(X * ZH, low, slab)
    targets = lax.all_to_all(targets, ("x", "zh"), 0, 0).reshape(X, ZH, low, slab)
    targets = targets.transpose(1, 2, 0, 3).reshape(ZH * low, columns).astype(jnp.float32)

    partial = jnp.dot(gathered, fc_flat, preferred_element_type=jnp.float32)
    partial = partial.reshape(Y, ZH, X, low, width)
    partial = pick(partial, core, 1) + swap(pick(partial, 1 - core, 1))
    partial = jnp.sum(lax.all_to_all(partial, "x", 1, 0), axis=0)
    joined_own = partial.reshape(Y * low, width).astype(jnp.bfloat16)
    joined_wide = spread(joined_own, DEPTH, Z).transpose(1, 0, 2).reshape(Y * low, depth)
    joined_pair = both_cores(joined_wide)

    logits = jnp.dot(
        joined_pair.reshape(ZH * Y * low, depth), head, preferred_element_type=jnp.float32
    )
    logits = lax.all_to_all(logits.reshape(ZH, Y, low, columns), "y", 1, 0)
    logits = jnp.sum(logits, axis=0).reshape(ZH * low, columns)

    next_segment = jnp.concatenate([segment_ids[1:], jnp.full((1,), -1, jnp.int32)])
    kept_all = loss_mask * (segment_ids == next_segment).astype(jnp.int32)
    kept_count = jnp.maximum(jnp.sum(kept_all), 1).astype(jnp.float32)

    def own(value):
        value = pick(value.reshape(Y, ZH, X, low), y, 0)
        return pick(value, x, 1).reshape(ZH * low)

    kept_tokens = own(kept_all).astype(jnp.float32)
    labels = vocab_map[own(token_ids)]
    lane = jnp.arange(columns, dtype=jnp.int32)
    vocab_id = (((lane // slab * C + core) * ZL + zl) * ZH + zh) * slab + lane % slab
    onehot = (labels[:, None] == vocab_id[None, :]).astype(jnp.float32)

    local_max = jnp.max(logits, axis=1)
    local_total = jnp.sum(jnp.exp(logits - local_max[:, None]), axis=1)
    picked = jnp.sum(onehot * logits, axis=1)
    dotted = jnp.sum(targets * logits, axis=1)
    prob_mass = jnp.sum(targets, axis=1)
    stats = jnp.stack([local_max, local_total, dotted, prob_mass, picked])
    stats = spread(stats, ("core", "zh", "zl"), C * Z)
    row_peak = jnp.max(stats[:, 0], axis=0)
    exp_total = jnp.sum(stats[:, 1] * jnp.exp(stats[:, 0] - row_peak), axis=0)
    dotted, prob_mass, picked = jnp.sum(stats[:, 2:], axis=0)
    log_total = row_peak + jnp.log(exp_total)
    token_loss = kept_tokens * (log_total * prob_mass - dotted + log_total - picked)
    loss_part = jnp.sum(token_loss) / kept_count / (C * Z)
    draft_probs = jnp.exp(logits - log_total[:, None])
    dlogits = (
        kept_tokens[:, None] * (draft_probs * (prob_mass[:, None] + 1.0) - targets - onehot)
    ).astype(jnp.bfloat16)

    shard = spread(dlogits, "y", Y).reshape(Y, ZH, low, columns)

    def feature(side):
        side = pick(shard, side, 1).reshape(Y * low, columns)
        return lax.dot_general(side, head, (((1,), (1,)), ((), ())), preferred_element_type=jnp.float32)

    theirs = swap(feature(1 - core))
    feature_part = feature(core) + theirs
    feature_part = lax.all_to_all(feature_part.reshape(Y * low, Z, width), DEPTH, 1, 0)
    feature_own = jnp.sum(feature_part, axis=0).astype(jnp.bfloat16)
    feature_all = both_cores(spread(feature_own, "x", X))
    feature_all = feature_all.reshape(ZH, X, Y, low, width).transpose(2, 0, 1, 3, 4)
    feature_all = feature_all.reshape(tokens, width)
    fc_grad = lax.dot_general(
        gathered, feature_all, (((0,), (0,)), ((), ())), preferred_element_type=jnp.float32
    )

    joined_all = both_cores(spread(joined_wide, "x", X)).reshape(tokens, depth)
    dlogits_all = lax.all_to_all(shard.reshape(Y, ZH, low, X, slab), "x", 3, 0)
    dlogits_all = dlogits_all.transpose(2, 0, 1, 3, 4).reshape(tokens, slab)
    head_grad = lax.dot_general(
        joined_all, dlogits_all, (((0,), (0,)), ((), ())), preferred_element_type=jnp.float32
    )
    squares = jnp.sum(head_grad * head_grad) + jnp.sum(fc_grad * fc_grad)
    head_grad = lax.all_to_all(head_grad.reshape(Z, width, slab), DEPTH, 0, 0)
    head_grad = head_grad.reshape(ZH, ZL, width, slab).transpose(2, 1, 0, 3).reshape(width, -1)

    sums = jnp.stack([squares, loss_part])
    sums = jnp.sum(spread(sums, ("x", "core"), X * C), axis=0)
    sums = jnp.sum(spread(sums, ("y", "zh", "zl"), Y * Z), axis=0)
    entries = 3.0 * D * D + 1.0 * D * VD
    scale = lax.rsqrt(sums[0] / entries + 1e-06)
    return ((fc_grad * scale).reshape(fc_weight.shape), head_grad * scale, sums[1])


def solution(mesh):
    fine = Mesh(mesh.devices.reshape(X, C, Y, ZH, ZL), ("x", "core", "y", "zh", "zl"))
    tgt, dp, vocab = ("x", "core"), ("y", "zh"), ("zl",)
    in_specs = (
        P(None, dp, tgt),
        P(None, tgt, dp + vocab),
        P(dp + vocab, tgt),
        P(dp, tgt + vocab),
        P(),
        P(),
        P(),
        P(),
    )
    out_specs = (P(None, tgt, dp + vocab), P(dp + vocab, tgt), P())
    return jax.shard_map(
        per_device, mesh=fine, in_specs=in_specs, out_specs=out_specs, check_vma=False
    )
```

```python
import jax
import jax.numpy as jnp
from jax import lax
from jax.sharding import Mesh, PartitionSpec as P

D = 8192
VD = 16384
X, C, Y, ZH, ZL = 4, 2, 4, 2, 4
Z = ZH * ZL
DEPTH = ("zh", "zl")


def spread(value, axes, count):
    return lax.all_to_all(jnp.broadcast_to(value[None], (count,) + value.shape), axes, 0, 0)


def swap(value):
    return lax.ppermute(value, "core", [(0, 1), (1, 0)])


def shift(value, axis, by):
    return lax.ppermute(value, axis, [(i, (i + by) % 4) for i in range(4)])


def pick(value, index, axis):
    return lax.dynamic_index_in_dim(value, index, axis, keepdims=False)


def chain(value, step, starts):
    hops = []
    for hop in range(4):
        pairs = [((s + step * hop) % Z, (s + step * (hop + 1)) % Z) for s in starts]
        value = lax.ppermute(value, DEPTH, pairs)
        hops.append(value)
    return hops


def rows_along_y(own):
    half = own.shape[0] // 2
    below, above = shift(own, "y", 1), shift(own, "y", -1)
    far = [shift(below[:half], "y", 1), shift(above[half:], "y", -1)]
    return jnp.concatenate([own, below, above] + far)


def total(value):
    value = value + swap(value)
    for axis in ("x", "y"):
        value = (value + shift(value, axis, 2)) + (shift(value, axis, 1) + shift(value, axis, -1))
    for bit in (1, 2, 4):
        value = value + lax.ppermute(value, DEPTH, [(i, i ^ bit) for i in range(Z)])
    return value


def per_device(
    hidden_rows, fc_weight, head_weight, target_probs, token_ids, vocab_map, segment_ids, loss_mask
):
    x, core, y = lax.axis_index("x"), lax.axis_index("core"), lax.axis_index("y")
    zh, zl = lax.axis_index("zh"), lax.axis_index("zl")
    rows = hidden_rows.shape[1]
    half = rows // 2
    tokens = rows * Y * ZH
    low = rows // X
    width = fc_weight.shape[2]
    depth = width * Z
    slab = head_weight.shape[1] // Z
    columns = slab * X
    same_side = core == zh
    near_low = zl < ZL // 2

    head = head_weight.reshape(width, ZL, ZH, slab).transpose(2, 1, 0, 3).reshape(Z, width, slab)
    head = lax.all_to_all(head, DEPTH, 0, 0).reshape(depth, slab)

    flat = hidden_rows.transpose(1, 0, 2).reshape(rows, -1)
    up = chain(flat[:half], 1, (ZL - 1, Z - 1))
    down = chain(flat[half:], -1, (ZL, 0))
    rows_own = rows_along_y(flat)
    first = jnp.where(zl == 0, up[0], jnp.where(zl == 1, up[1], jnp.where(zl == 2, down[1], down[0])))
    second = jnp.where(zl == 0, down[3], jnp.where(zl == 1, down[2], jnp.where(zl == 2, up[2], up[3])))
    rows_first = rows_along_y(first)
    second, head = lax.optimization_barrier((second, head))
    head = lax.all_gather(head, "x", axis=1, tiled=True)
    rows_second = rows_along_y(second)
    gathered = jnp.concatenate([rows_own, rows_first, rows_second])
    fc_flat = fc_weight.reshape(-1, width)

    targets = target_probs.reshape(X, low, ZH, slab).transpose(0, 2, 1, 3)
    targets = targets.reshape(X * ZH, low, slab)
    targets = lax.all_to_all(targets, ("x", "zh"), 0, 0).reshape(X, ZH, low, slab)
    targets = targets.transpose(1, 2, 0, 3).reshape(ZH * low, columns).astype(jnp.float32)

    def join(part):
        part = jnp.dot(part, fc_flat, preferred_element_type=jnp.float32)
        return part.reshape(Y, -1, width)

    part_own, part_first, part_second = join(rows_own), join(rows_first), join(rows_second)
    part_other = jnp.concatenate(
        [
            jnp.where(near_low, part_first, part_second),
            jnp.where(near_low, part_second, part_first),
        ],
        axis=1,
    )
    theirs = swap(jnp.where(same_side, part_other, part_own))
    partial = jnp.where(same_side, part_own, part_other) + theirs
    partial = partial.reshape(Y, X, low, width)
    joined_own = pick(partial, x, 1)
    for by in (1, -1, 2):
        joined_own = joined_own + shift(pick(partial, (x + by) % X, 1), "x", by)
    joined_own = joined_own.reshape(Y * low, width).astype(jnp.bfloat16)
    joined_wide = spread(joined_own, DEPTH, Z).transpose(1, 0, 2).reshape(Y * low, depth)
    mine, theirs = joined_wide.reshape(Y, low, depth), swap(joined_wide).reshape(Y, low, depth)
    joined_pair = jnp.stack(
        [jnp.where(core == 0, mine, theirs), jnp.where(core == 0, theirs, mine)], axis=1
    )

    partial = jnp.dot(
        joined_pair.reshape(Y * ZH * low, depth), head, preferred_element_type=jnp.float32
    )
    partial = partial.reshape(Y, ZH * low, columns)
    logits = partial[0]
    for place, by in ((1, -1), (2, 1), (3, 2)):
        logits = logits + shift(partial[place], "y", by)

    next_segment = jnp.concatenate([segment_ids[1:], jnp.full((1,), -1, jnp.int32)])
    kept_all = loss_mask * (segment_ids == next_segment).astype(jnp.int32)
    kept_count = jnp.maximum(jnp.sum(kept_all), 1).astype(jnp.float32)

    def own(value):
        value = pick(value.reshape(Y, ZH, X, low), y, 0)
        return pick(value, x, 1).reshape(ZH * low)

    kept_tokens = own(kept_all).astype(jnp.float32)
    labels = vocab_map[own(token_ids)]
    lane = jnp.arange(columns, dtype=jnp.int32)
    vocab_id = (((lane // slab * C + core) * ZL + zl) * ZH + zh) * slab + lane % slab
    onehot = (labels[:, None] == vocab_id[None, :]).astype(jnp.float32)

    local_max = jnp.max(logits, axis=1)
    local_total = jnp.sum(jnp.exp(logits - local_max[:, None]), axis=1)
    picked = jnp.sum(onehot * logits, axis=1)
    dotted = jnp.sum(targets * logits, axis=1)
    prob_mass = jnp.sum(targets, axis=1)
    stats = jnp.stack([local_max, local_total, dotted, prob_mass, picked])
    stats = spread(stats, ("core", "zh", "zl"), C * Z)
    row_peak = jnp.max(stats[:, 0], axis=0)
    exp_total = jnp.sum(stats[:, 1] * jnp.exp(stats[:, 0] - row_peak), axis=0)
    dotted, prob_mass, picked = jnp.sum(stats[:, 2:], axis=0)
    log_total = row_peak + jnp.log(exp_total)
    token_loss = kept_tokens * (log_total * prob_mass - dotted + log_total - picked)
    loss_part = jnp.sum(token_loss) / kept_count / (C * Z)
    draft_probs = jnp.exp(logits - log_total[:, None])
    dlogits = (
        kept_tokens[:, None] * (draft_probs * (prob_mass[:, None] + 1.0) - targets - onehot)
    ).astype(jnp.bfloat16)

    shard = jnp.stack([dlogits] + [shift(dlogits, "y", by) for by in (1, -1, 2)])
    shard = shard.reshape(Y, ZH, low, columns)

    def feature(side):
        side = pick(shard, side, 1).reshape(Y * low, columns)
        return lax.dot_general(side, head, (((1,), (1,)), ((), ())), preferred_element_type=jnp.float32)

    theirs = swap(feature(1 - core))
    feature_part = feature(core) + theirs
    feature_part = lax.all_to_all(feature_part.reshape(Y * low, Z, width), DEPTH, 1, 0)
    feature_own = jnp.sum(feature_part, axis=0).astype(jnp.bfloat16)
    ring = [feature_own] + [shift(feature_own, "x", by) for by in (-1, 2, 1)]
    ring = lax.dynamic_slice_in_dim(jnp.stack(ring + ring[:-1]), (X - x) % X, X, 0)
    ring = ring.reshape(X, Y, low, width).transpose(1, 0, 2, 3)
    other = swap(ring)
    feature_near = jnp.where(same_side, ring, other).reshape(Y * rows, width)
    feature_far = jnp.where(same_side, other, ring).reshape(Y, 2, half, width)
    feature_far = [feature_far[:, 0].reshape(-1, width), feature_far[:, 1].reshape(-1, width)]
    feature_all = jnp.concatenate(
        [
            feature_near,
            jnp.where(near_low, feature_far[0], feature_far[1]),
            jnp.where(near_low, feature_far[1], feature_far[0]),
        ]
    )
    fc_grad = lax.dot_general(
        gathered, feature_all, (((0,), (0,)), ((), ())), preferred_element_type=jnp.float32
    )

    joined_all = lax.all_gather(joined_wide, ("x", "core"), axis=0, tiled=True)
    dlogits_all = lax.all_to_all(shard.reshape(Y, ZH, low, X, slab), "x", 3, 0)
    dlogits_all = dlogits_all.transpose(0, 2, 1, 3, 4).reshape(tokens, slab)
    head_grad = lax.dot_general(
        joined_all, dlogits_all, (((0,), (0,)), ((), ())), preferred_element_type=jnp.float32
    )
    squares = jnp.sum(head_grad * head_grad) + jnp.sum(fc_grad * fc_grad)
    head_grad = lax.all_to_all(head_grad.reshape(Z, width, slab), DEPTH, 0, 0)
    head_grad = head_grad.reshape(ZH, ZL, width, slab).transpose(2, 1, 0, 3).reshape(width, -1)

    sums = total(jnp.stack([squares, loss_part]))
    entries = 3.0 * D * D + 1.0 * D * VD
    scale = lax.rsqrt(sums[0] / entries + 1e-06)
    return ((fc_grad * scale).reshape(fc_weight.shape), head_grad * scale, sums[1])


def solution(mesh):
    fine = Mesh(mesh.devices.reshape(X, C, Y, ZH, ZL), ("x", "core", "y", "zh", "zl"))
    tgt, dp, vocab = ("x", "core"), ("y", "zh"), ("zl",)
    in_specs = (
        P(None, dp, tgt),
        P(None, tgt, dp + vocab),
        P(dp + vocab, tgt),
        P(dp, tgt + vocab),
        P(),
        P(),
        P(),
        P(),
    )
    out_specs = (P(None, tgt, dp + vocab), P(dp + vocab, tgt), P())
    return jax.shard_map(
        per_device, mesh=fine, in_specs=in_specs, out_specs=out_specs, check_vma=False
    )
```

```python
import jax
import jax.numpy as jnp
from jax import lax
from jax.experimental import pallas as pl
from jax.experimental.pallas import tpu as pltpu
from jax.sharding import Mesh, PartitionSpec as P

D = 8192
VD = 16384
X, C, Y, ZH, ZL = 4, 2, 4, 2, 4
Z = ZH * ZL
DEPTH = ("zh", "zl")


def spread(value, axes, count):
    return lax.all_to_all(jnp.broadcast_to(value[None], (count,) + value.shape), axes, 0, 0)


def swap(value):
    return lax.ppermute(value, "core", [(0, 1), (1, 0)])


def shift(value, axis, by):
    return lax.ppermute(value, axis, [(i, (i + by) % 4) for i in range(4)])


def pick(value, index, axis):
    return lax.dynamic_index_in_dim(value, index, axis, keepdims=False)


def arrange(parts):
    out = jnp.zeros((len(parts),) + parts[0][1].shape, parts[0][1].dtype)
    for index, part in parts:
        out = lax.dynamic_update_index_in_dim(out, part, index, 0)
    return out


def fc_kernel(near_ref, far_ref, feature_ref, out_ref, squares_ref):
    row = 0
    acc = None
    for ref in (near_ref, far_ref):
        rows = ref.shape[0]
        term = lax.dot_general(
            ref[...],
            feature_ref[row : row + rows, :],
            (((0,), (0,)), ((), ())),
            preferred_element_type=jnp.float32,
        )
        acc = term if acc is None else acc + term
        row += rows
    out_ref[...] = acc

    @pl.when(pl.program_id(0) == 0)
    def _():
        squares_ref[...] = jnp.zeros_like(squares_ref)

    squares_ref[...] += jnp.sum(acc * acc, axis=0, keepdims=True)


def fc_product(near, far, feature):
    block = 512
    deep, width = near.shape[1], feature.shape[1]
    out, squares = pl.pallas_call(
        fc_kernel,
        grid=(deep // block,),
        in_specs=[
            pl.BlockSpec((part.shape[0], block), lambda i: (0, i)) for part in (near, far)
        ]
        + [pl.BlockSpec(feature.shape, lambda i: (0, 0))],
        out_specs=[
            pl.BlockSpec((block, width), lambda i: (i, 0)),
            pl.BlockSpec((1, width), lambda i: (0, 0)),
        ],
        out_shape=[
            jax.ShapeDtypeStruct((deep, width), jnp.float32),
            jax.ShapeDtypeStruct((1, width), jnp.float32),
        ],
        compiler_params=pltpu.CompilerParams(
            dimension_semantics=("arbitrary",), vmem_limit_bytes=24 * 1024 * 1024
        ),
        cost_estimate=pl.CostEstimate(
            flops=2 * feature.shape[0] * deep * width, bytes_accessed=10 * 2**20, transcendentals=0
        ),
    )(near, far, feature)
    return out, jnp.sum(squares)


def scale_kernel(scale_ref, value_ref, out_ref):
    out_ref[...] = value_ref[0] * scale_ref[0, 0]


def scaled_columns(value, scale):
    _, width, slab = value.shape
    return pl.pallas_call(
        scale_kernel,
        grid=(Z,),
        in_specs=[
            pl.BlockSpec(memory_space=pltpu.SMEM),
            pl.BlockSpec((1, width, slab), lambda i: ((i % ZH) * ZL + i // ZH, 0, 0)),
        ],
        out_specs=pl.BlockSpec((width, slab), lambda i: (0, i)),
        out_shape=jax.ShapeDtypeStruct((width, Z * slab), jnp.float32),
        cost_estimate=pl.CostEstimate(
            flops=value.size, bytes_accessed=8 * value.size, transcendentals=0
        ),
    )(scale.reshape(1, 1), value)


def total(value):
    value = value + swap(value)
    for axis in ("x", "y"):
        value = (value + shift(value, axis, 2)) + (shift(value, axis, 1) + shift(value, axis, -1))
    for bit in (1, 2, 4):
        value = value + lax.ppermute(value, DEPTH, [(i, i ^ bit) for i in range(Z)])
    return value


def per_device(
    hidden_rows, fc_weight, head_weight, target_probs, token_ids, vocab_map, segment_ids, loss_mask
):
    x, core, y = lax.axis_index("x"), lax.axis_index("core"), lax.axis_index("y")
    zh, zl = lax.axis_index("zh"), lax.axis_index("zl")
    rows = hidden_rows.shape[1]
    tokens = rows * Y * ZH
    low = rows // X
    width = fc_weight.shape[2]
    depth = width * Z
    slab = head_weight.shape[1] // Z
    columns = slab * X
    same_side = core == zh

    flat = hidden_rows.transpose(1, 0, 2).reshape(rows, -1)
    far = lax.ppermute(flat, "zh", [(0, 1), (1, 0)])
    rows_near = lax.all_gather(flat, "y", axis=0, tiled=True)
    rows_far = lax.all_gather(far, "y", axis=0, tiled=True)

    head = head_weight.reshape(width, ZL, ZH, slab).transpose(2, 1, 0, 3).reshape(Z, width, slab)
    head, _ = lax.optimization_barrier((head, far))
    head = lax.all_to_all(head, DEPTH, 0, 0).reshape(depth, slab)

    targets = target_probs.reshape(X, low, ZH, slab).transpose(0, 2, 1, 3)
    targets = targets.reshape(X * ZH, low, slab)
    targets, head = lax.optimization_barrier((targets, head))
    targets = lax.all_to_all(targets, ("x", "zh"), 0, 0).reshape(X, ZH, low, slab)
    targets, rows_near = lax.optimization_barrier((targets, rows_near))

    head = lax.all_gather(head, "x", axis=1, tiled=True)
    targets = targets.transpose(1, 2, 0, 3).reshape(ZH * low, columns).astype(jnp.float32)
    fc_flat = fc_weight.reshape(-1, width)

    part_near = jnp.dot(rows_near, fc_flat, preferred_element_type=jnp.float32)
    part_far = jnp.dot(rows_far, fc_flat, preferred_element_type=jnp.float32)
    theirs = swap(jnp.where(same_side, part_far, part_near))
    partial = jnp.where(same_side, part_near, part_far) + theirs
    partial = partial.reshape(Y, X, low, width)
    joined_own = pick(partial, x, 1)
    for by in (1, -1, 2):
        joined_own = joined_own + shift(pick(partial, (x + by) % X, 1), "x", by)
    joined_own = joined_own.reshape(Y * low, width).astype(jnp.bfloat16)
    joined_wide = spread(joined_own, DEPTH, Z).transpose(1, 0, 2).reshape(Y * low, depth)
    mine, theirs = joined_wide.reshape(Y, low, depth), swap(joined_wide).reshape(Y, low, depth)
    joined_pair = jnp.stack(
        [jnp.where(core == 0, mine, theirs), jnp.where(core == 0, theirs, mine)], axis=1
    )

    partial = jnp.dot(
        joined_pair.reshape(Y * ZH * low, depth), head, preferred_element_type=jnp.float32
    )
    partial = partial.reshape(Y, ZH * low, columns)
    logits = pick(partial, y, 0)
    for by in (1, -1, 2):
        logits = logits + shift(pick(partial, (y + by) % Y, 0), "y", by)

    next_segment = jnp.concatenate([segment_ids[1:], jnp.full((1,), -1, jnp.int32)])
    kept_all = loss_mask * (segment_ids == next_segment).astype(jnp.int32)
    kept_count = jnp.maximum(jnp.sum(kept_all), 1).astype(jnp.float32)

    def own(value):
        value = pick(value.reshape(Y, ZH, X, low), y, 0)
        return pick(value, x, 1).reshape(ZH * low)

    kept_tokens = own(kept_all).astype(jnp.float32)
    labels = vocab_map[own(token_ids)]
    lane = jnp.arange(columns, dtype=jnp.int32)
    vocab_id = (((lane // slab * C + core) * ZL + zl) * ZH + zh) * slab + lane % slab
    onehot = (labels[:, None] == vocab_id[None, :]).astype(jnp.float32)

    local_max = jnp.max(logits, axis=1)
    local_total = jnp.sum(jnp.exp(logits - local_max[:, None]), axis=1)
    picked = jnp.sum(onehot * logits, axis=1)
    dotted = jnp.sum(targets * logits, axis=1)
    prob_mass = jnp.sum(targets, axis=1)
    stats = jnp.stack([local_max, local_total, dotted, prob_mass, picked])
    stats = spread(stats, ("core", "zh", "zl"), C * Z)
    row_peak = jnp.max(stats[:, 0], axis=0)
    exp_total = jnp.sum(stats[:, 1] * jnp.exp(stats[:, 0] - row_peak), axis=0)
    dotted, prob_mass, picked = jnp.sum(stats[:, 2:], axis=0)
    log_total = row_peak + jnp.log(exp_total)
    token_loss = kept_tokens * (log_total * prob_mass - dotted + log_total - picked)
    loss_part = jnp.sum(token_loss) / kept_count / (C * Z)
    draft_probs = jnp.exp(logits - log_total[:, None])
    dlogits = (
        kept_tokens[:, None] * (draft_probs * (prob_mass[:, None] + 1.0) - targets - onehot)
    ).astype(jnp.bfloat16)

    shard = [(y, dlogits)] + [((y - by) % Y, shift(dlogits, "y", by)) for by in (1, -1, 2)]
    shard = arrange(shard).reshape(Y, ZH, low, columns)

    def feature(side):
        side = pick(shard, side, 1).reshape(Y * low, columns)
        return lax.dot_general(side, head, (((1,), (1,)), ((), ())), preferred_element_type=jnp.float32)

    theirs = swap(feature(1 - core))
    feature_part = feature(core) + theirs
    feature_part = lax.all_to_all(feature_part.reshape(Y * low, Z, width), DEPTH, 1, 0)
    feature_own = jnp.sum(feature_part, axis=0).astype(jnp.bfloat16)
    ring = [(x, feature_own)]
    ring += [((x - by) % X, shift(feature_own, "x", by)) for by in (1, -1, 2)]
    ring = arrange(ring).reshape(X, Y, low, width).transpose(1, 0, 2, 3)
    other = swap(ring)
    feature_all = jnp.concatenate([jnp.where(same_side, ring, other), jnp.where(same_side, other, ring)])
    feature_all = feature_all.reshape(tokens, width)
    fc_grad, fc_squares = fc_product(rows_near, rows_far, feature_all)

    joined_all = lax.all_gather(joined_wide, ("x", "core"), axis=0, tiled=True)
    dlogits_all = lax.all_to_all(shard.reshape(Y, ZH, low, X, slab), "x", 3, 0)
    dlogits_all = dlogits_all.transpose(0, 2, 1, 3, 4).reshape(tokens, slab)
    head_grad = lax.dot_general(
        joined_all, dlogits_all, (((0,), (0,)), ((), ())), preferred_element_type=jnp.float32
    )
    squares = jnp.sum(head_grad * head_grad) + fc_squares
    head_grad = lax.all_to_all(head_grad.reshape(Z, width, slab), DEPTH, 0, 0)

    sums = total(jnp.stack([squares, loss_part]))
    entries = 3.0 * D * D + 1.0 * D * VD
    scale = lax.rsqrt(sums[0] / entries + 1e-06)
    return ((fc_grad * scale).reshape(fc_weight.shape), scaled_columns(head_grad, scale), sums[1])


def solution(mesh):
    fine = Mesh(mesh.devices.reshape(X, C, Y, ZH, ZL), ("x", "core", "y", "zh", "zl"))
    tgt, dp, vocab = ("x", "core"), ("y", "zh"), ("zl",)
    in_specs = (
        P(None, dp, tgt),
        P(None, tgt, dp + vocab),
        P(dp + vocab, tgt),
        P(dp, tgt + vocab),
        P(),
        P(),
        P(),
        P(),
    )
    out_specs = (P(None, tgt, dp + vocab), P(dp + vocab, tgt), P())
    return jax.shard_map(
        per_device, mesh=fine, in_specs=in_specs, out_specs=out_specs, check_vma=False
    )
```

```python
import jax
import jax.numpy as jnp
from jax import lax
from jax.experimental import pallas as pl
from jax.experimental.pallas import tpu as pltpu
from jax.sharding import Mesh, PartitionSpec as P

D = 8192
VD = 16384
X, C, Y, ZH, ZL = 4, 2, 4, 2, 4
Z = ZH * ZL
DEPTH = ("zh", "zl")


def spread(value, axes, count):
    return lax.all_to_all(jnp.broadcast_to(value[None], (count,) + value.shape), axes, 0, 0)


def swap(value):
    return lax.ppermute(value, "core", [(0, 1), (1, 0)])


def shift(value, axis, by):
    return lax.ppermute(value, axis, [(i, (i + by) % 4) for i in range(4)])


def pick(value, index, axis):
    return lax.dynamic_index_in_dim(value, index, axis, keepdims=False)


def arrange(parts):
    out = jnp.zeros((len(parts),) + parts[0][1].shape, parts[0][1].dtype)
    for index, part in parts:
        out = lax.dynamic_update_index_in_dim(out, part, index, 0)
    return out


VMEM_BYTES = 56 * 1024 * 1024


def kernel_params():
    return pltpu.CompilerParams(
        dimension_semantics=("arbitrary",), vmem_limit_bytes=VMEM_BYTES
    )


def fc_kernel(*refs):
    row_refs, (feature_ref, out_ref, squares_ref) = refs[:-3], refs[-3:]
    row = 0
    acc = None
    for ref in row_refs:
        rows = ref.shape[0]
        term = lax.dot_general(
            ref[...],
            feature_ref[row : row + rows, :],
            (((0,), (0,)), ((), ())),
            preferred_element_type=jnp.float32,
        )
        acc = term if acc is None else acc + term
        row += rows
    out_ref[...] = acc

    @pl.when(pl.program_id(0) == 0)
    def _():
        squares_ref[...] = jnp.zeros_like(squares_ref)

    squares_ref[...] += jnp.sum(acc * acc, axis=0, keepdims=True)


def fc_product(groups, feature):
    block = 512
    deep, width = groups[0].shape[1], feature.shape[1]
    out, squares = pl.pallas_call(
        fc_kernel,
        grid=(deep // block,),
        in_specs=[pl.BlockSpec((part.shape[0], block), lambda i: (0, i)) for part in groups]
        + [pl.BlockSpec(feature.shape, lambda i: (0, 0))],
        out_specs=[
            pl.BlockSpec((block, width), lambda i: (i, 0)),
            pl.BlockSpec((1, width), lambda i: (0, 0)),
        ],
        out_shape=[
            jax.ShapeDtypeStruct((deep, width), jnp.float32),
            jax.ShapeDtypeStruct((1, width), jnp.float32),
        ],
        compiler_params=kernel_params(),
        cost_estimate=pl.CostEstimate(
            flops=2 * feature.shape[0] * deep * width, bytes_accessed=10 * 2**20, transcendentals=0
        ),
    )(*groups, feature)
    return out, jnp.sum(squares)


def head_kernel(joined_ref, value_ref, out_ref, squares_ref):
    acc = lax.dot_general(
        joined_ref[...],
        value_ref[...],
        (((0,), (0,)), ((), ())),
        preferred_element_type=jnp.float32,
    )
    out_ref[0] = acc

    @pl.when(pl.program_id(0) == 0)
    def _():
        squares_ref[...] = jnp.zeros_like(squares_ref)

    squares_ref[...] += jnp.sum(acc * acc, axis=0, keepdims=True)


def head_product(joined, value):
    rows, depth = joined.shape
    width, slab = depth // Z, value.shape[1]
    out, squares = pl.pallas_call(
        head_kernel,
        grid=(Z,),
        in_specs=[
            pl.BlockSpec((rows, width), lambda i: (0, i)),
            pl.BlockSpec(value.shape, lambda i: (0, 0)),
        ],
        out_specs=[
            pl.BlockSpec((1, width, slab), lambda i: (i, 0, 0)),
            pl.BlockSpec((1, slab), lambda i: (0, 0)),
        ],
        out_shape=[
            jax.ShapeDtypeStruct((Z, width, slab), jnp.float32),
            jax.ShapeDtypeStruct((1, slab), jnp.float32),
        ],
        compiler_params=kernel_params(),
        cost_estimate=pl.CostEstimate(
            flops=2 * rows * depth * slab, bytes_accessed=7 * 2**20, transcendentals=0
        ),
    )(joined, value)
    return out, jnp.sum(squares)


def scale_kernel(scale_ref, fc_ref, head_ref, fc_out_ref, head_out_ref):
    scale = scale_ref[0, 0]
    slab = head_ref.shape[3]
    fc_out_ref[...] = fc_ref[...] * scale
    for side in range(ZH):
        head_out_ref[:, side * slab : (side + 1) * slab] = head_ref[side, 0] * scale


def scaled(fc_grad, head_grad, scale):
    deep, width = fc_grad.shape
    _, _, rows, slab = head_grad.shape
    return pl.pallas_call(
        scale_kernel,
        grid=(ZL,),
        in_specs=[
            pl.BlockSpec(memory_space=pltpu.SMEM),
            pl.BlockSpec((deep // ZL, width), lambda i: (i, 0)),
            pl.BlockSpec((ZH, 1, rows, slab), lambda i: (0, i, 0, 0)),
        ],
        out_specs=[
            pl.BlockSpec((deep // ZL, width), lambda i: (i, 0)),
            pl.BlockSpec((rows, ZH * slab), lambda i: (0, i)),
        ],
        out_shape=[
            jax.ShapeDtypeStruct(fc_grad.shape, jnp.float32),
            jax.ShapeDtypeStruct((rows, Z * slab), jnp.float32),
        ],
        compiler_params=kernel_params(),
        cost_estimate=pl.CostEstimate(
            flops=fc_grad.size + head_grad.size,
            bytes_accessed=8 * (fc_grad.size + head_grad.size),
            transcendentals=0,
        ),
    )(scale.reshape(1, 1), fc_grad, head_grad)


def total(value):
    value = value + swap(value)
    for axis in ("x", "y"):
        value = (value + shift(value, axis, 2)) + (shift(value, axis, 1) + shift(value, axis, -1))
    for bit in (1, 2, 4):
        value = value + lax.ppermute(value, DEPTH, [(i, i ^ bit) for i in range(Z)])
    return value


def per_device(
    hidden_rows, fc_weight, head_weight, target_probs, token_ids, vocab_map, segment_ids, loss_mask
):
    x, core, y = lax.axis_index("x"), lax.axis_index("core"), lax.axis_index("y")
    zh, zl = lax.axis_index("zh"), lax.axis_index("zl")
    rows = hidden_rows.shape[1]
    tokens = rows * Y * ZH
    low = rows // X
    width = fc_weight.shape[2]
    depth = width * Z
    slab = head_weight.shape[1] // Z
    columns = slab * X
    same_side = core == zh

    flat = hidden_rows.transpose(1, 0, 2).reshape(rows, -1)
    far = lax.ppermute(flat, "zh", [(0, 1), (1, 0)])
    rows_near = lax.all_gather(flat, "y", axis=0, tiled=True)
    rows_far = lax.all_gather(far, "y", axis=0, tiled=True)

    head = head_weight.reshape(width, ZL, ZH, slab).transpose(2, 1, 0, 3).reshape(Z, width, slab)
    head, _ = lax.optimization_barrier((head, far))
    head = lax.all_to_all(head, DEPTH, 0, 0).reshape(depth, slab)

    targets = target_probs.reshape(X, low, ZH, slab).transpose(0, 2, 1, 3)
    targets = targets.reshape(X * ZH, low, slab)
    targets, head = lax.optimization_barrier((targets, head))
    targets = lax.all_to_all(targets, ("x", "zh"), 0, 0).reshape(X, ZH, low, slab)
    targets, rows_near = lax.optimization_barrier((targets, rows_near))

    head = lax.all_gather(head, "x", axis=1, tiled=True)
    targets = targets.transpose(1, 2, 0, 3).reshape(ZH * low, columns).astype(jnp.float32)
    fc_flat = fc_weight.reshape(-1, width)

    part_near = jnp.dot(rows_near, fc_flat, preferred_element_type=jnp.float32)
    part_far = jnp.dot(rows_far, fc_flat, preferred_element_type=jnp.float32)
    theirs = swap(jnp.where(same_side, part_far, part_near))
    partial = jnp.where(same_side, part_near, part_far) + theirs
    partial = partial.reshape(Y, X, low, width)
    joined_own = pick(partial, x, 1)
    for by in (1, -1, 2):
        joined_own = joined_own + shift(pick(partial, (x + by) % X, 1), "x", by)
    joined_own = joined_own.reshape(Y * low, width).astype(jnp.bfloat16)
    joined_wide = spread(joined_own, DEPTH, Z).transpose(1, 0, 2).reshape(Y * low, depth)
    mine, theirs = joined_wide.reshape(Y, low, depth), swap(joined_wide).reshape(Y, low, depth)
    joined_all = lax.all_gather(joined_wide, ("x", "core"), axis=0, tiled=True)
    joined_pair = jnp.stack(
        [jnp.where(core == 0, mine, theirs), jnp.where(core == 0, theirs, mine)], axis=1
    )

    partial = jnp.dot(
        joined_pair.reshape(Y * ZH * low, depth), head, preferred_element_type=jnp.float32
    )
    partial = partial.reshape(Y, ZH * low, columns)
    logits = pick(partial, y, 0)
    for by in (1, -1, 2):
        logits = logits + shift(pick(partial, (y + by) % Y, 0), "y", by)

    next_segment = jnp.concatenate([segment_ids[1:], jnp.full((1,), -1, jnp.int32)])
    kept_all = loss_mask * (segment_ids == next_segment).astype(jnp.int32)
    kept_count = jnp.maximum(jnp.sum(kept_all), 1).astype(jnp.float32)

    def own(value):
        value = pick(value.reshape(Y, ZH, X, low), y, 0)
        return pick(value, x, 1).reshape(ZH * low)

    kept_tokens = own(kept_all).astype(jnp.float32)
    labels = vocab_map[own(token_ids)]
    lane = jnp.arange(columns, dtype=jnp.int32)
    vocab_id = (((lane // slab * C + core) * ZL + zl) * ZH + zh) * slab + lane % slab
    onehot = (labels[:, None] == vocab_id[None, :]).astype(jnp.float32)

    local_max = jnp.max(logits, axis=1)
    local_total = jnp.sum(jnp.exp(logits - local_max[:, None]), axis=1)
    picked = jnp.sum(onehot * logits, axis=1)
    dotted = jnp.sum(targets * logits, axis=1)
    prob_mass = jnp.sum(targets, axis=1)
    stats = jnp.stack([local_max, local_total, dotted, prob_mass, picked])
    stats = spread(stats, ("core", "zh", "zl"), C * Z)
    row_peak = jnp.max(stats[:, 0], axis=0)
    exp_total = jnp.sum(stats[:, 1] * jnp.exp(stats[:, 0] - row_peak), axis=0)
    dotted, prob_mass, picked = jnp.sum(stats[:, 2:], axis=0)
    log_total = row_peak + jnp.log(exp_total)
    token_loss = kept_tokens * (log_total * prob_mass - dotted + log_total - picked)
    loss_part = jnp.sum(token_loss) / kept_count / (C * Z)
    draft_probs = jnp.exp(logits - log_total[:, None])
    dlogits = (
        kept_tokens[:, None] * (draft_probs * (prob_mass[:, None] + 1.0) - targets - onehot)
    ).astype(jnp.bfloat16)

    shard = [(y, dlogits)] + [((y - by) % Y, shift(dlogits, "y", by)) for by in (1, -1, 2)]
    shard = arrange(shard).reshape(Y, ZH, low, columns)
    shard, joined_all = lax.optimization_barrier((shard, joined_all))

    def feature(side):
        side = pick(shard, side, 1).reshape(Y * low, columns)
        return lax.dot_general(side, head, (((1,), (1,)), ((), ())), preferred_element_type=jnp.float32)

    theirs = swap(feature(1 - core))
    feature_part = feature(core) + theirs
    feature_part = lax.all_to_all(feature_part.reshape(Y * low, Z, width), DEPTH, 1, 0)

    dlogits_all = lax.all_gather(shard.reshape(-1, columns), "x", axis=0, tiled=True)
    dlogits_all = lax.dynamic_slice_in_dim(dlogits_all, x * slab, slab, 1)
    dlogits_all = dlogits_all.reshape(X, Y, ZH, low, slab).transpose(0, 2, 1, 3, 4)
    head_grad, head_squares = head_product(joined_all, dlogits_all.reshape(tokens, slab))
    feature_part, head_grad = lax.optimization_barrier((feature_part, head_grad))
    head_grad = lax.all_to_all(head_grad, DEPTH, 0, 0)

    feature_own = jnp.sum(feature_part, axis=0).astype(jnp.bfloat16)

    ring = [(x, feature_own)]
    ring += [((x - by) % X, shift(feature_own, "x", by)) for by in (1, -1, 2)]
    ring = arrange(ring).reshape(X, Y, low, width).transpose(1, 0, 2, 3)
    other = swap(ring)
    feature_all = jnp.stack([jnp.where(same_side, ring, other), jnp.where(same_side, other, ring)])
    fc_grad, fc_squares = fc_product([rows_near, rows_far], feature_all.reshape(tokens, width))

    sums = total(jnp.stack([head_squares + fc_squares, loss_part]))
    entries = 3.0 * D * D + 1.0 * D * VD
    scale = lax.rsqrt(sums[0] / entries + 1e-06)
    fc_step, head_step = scaled(fc_grad, head_grad.reshape(ZH, ZL, width, slab), scale)
    return (fc_step.reshape(fc_weight.shape), head_step, sums[1])


def solution(mesh):
    fine = Mesh(mesh.devices.reshape(X, C, Y, ZH, ZL), ("x", "core", "y", "zh", "zl"))
    tgt, dp, vocab = ("x", "core"), ("y", "zh"), ("zl",)
    in_specs = (
        P(None, dp, tgt),
        P(None, tgt, dp + vocab),
        P(dp + vocab, tgt),
        P(dp, tgt + vocab),
        P(),
        P(),
        P(),
        P(),
    )
    out_specs = (P(None, tgt, dp + vocab), P(dp + vocab, tgt), P())
    return jax.shard_map(
        per_device, mesh=fine, in_specs=in_specs, out_specs=out_specs, check_vma=False
    )
```

```python
import jax
import jax.numpy as jnp
from jax import lax
from jax.experimental import pallas as pl
from jax.experimental.pallas import tpu as pltpu
from jax.sharding import Mesh, PartitionSpec as P

D = 8192
VD = 16384
X, C, Y, ZH, ZL = 4, 2, 4, 2, 4
Z = ZH * ZL
DEPTH = ("zh", "zl")


def spread(value, axes, count):
    return lax.all_to_all(jnp.broadcast_to(value[None], (count,) + value.shape), axes, 0, 0)


def swap(value):
    return lax.ppermute(value, "core", [(0, 1), (1, 0)])


def shift(value, axis, by):
    return lax.ppermute(value, axis, [(i, (i + by) % 4) for i in range(4)])


def pick(value, index, axis):
    return lax.dynamic_index_in_dim(value, index, axis, keepdims=False)


def arrange(parts):
    out = jnp.zeros((len(parts),) + parts[0][1].shape, parts[0][1].dtype)
    for index, part in parts:
        out = lax.dynamic_update_index_in_dim(out, part, index, 0)
    return out


VMEM_BYTES = 56 * 1024 * 1024


def kernel_params():
    return pltpu.CompilerParams(
        dimension_semantics=("arbitrary",), vmem_limit_bytes=VMEM_BYTES
    )


def fc_kernel(*refs):
    row_refs, (feature_ref, out_ref, squares_ref) = refs[:-3], refs[-3:]
    row = 0
    acc = None
    for ref in row_refs:
        rows = ref.shape[0]
        term = lax.dot_general(
            ref[...],
            feature_ref[row : row + rows, :],
            (((0,), (0,)), ((), ())),
            preferred_element_type=jnp.float32,
        )
        acc = term if acc is None else acc + term
        row += rows
    out_ref[...] = acc

    @pl.when(pl.program_id(0) == 0)
    def _():
        squares_ref[...] = jnp.zeros_like(squares_ref)

    squares_ref[...] += jnp.sum(acc * acc, axis=0, keepdims=True)


def fc_product(groups, feature):
    block = 512
    deep, width = groups[0].shape[1], feature.shape[1]
    out, squares = pl.pallas_call(
        fc_kernel,
        grid=(deep // block,),
        in_specs=[
            pl.BlockSpec((part.shape[0] // 2, block), lambda i, half=half: (half, i))
            for part in groups
            for half in range(2)
        ]
        + [pl.BlockSpec(feature.shape, lambda i: (0, 0))],
        out_specs=[
            pl.BlockSpec((block, width), lambda i: (i, 0)),
            pl.BlockSpec((1, width), lambda i: (0, 0)),
        ],
        out_shape=[
            jax.ShapeDtypeStruct((deep, width), jnp.float32),
            jax.ShapeDtypeStruct((1, width), jnp.float32),
        ],
        compiler_params=kernel_params(),
        cost_estimate=pl.CostEstimate(
            flops=2 * feature.shape[0] * deep * width, bytes_accessed=10 * 2**20, transcendentals=0
        ),
    )(*[part for part in groups for _ in range(2)], feature)
    return out, squares


def head_kernel(joined_ref, value_ref, out_ref, squares_ref):
    acc = lax.dot_general(
        joined_ref[...],
        value_ref[...],
        (((0,), (0,)), ((), ())),
        preferred_element_type=jnp.float32,
    )
    out_ref[0] = acc

    @pl.when(pl.program_id(0) == 0)
    def _():
        squares_ref[...] = jnp.zeros_like(squares_ref)

    squares_ref[...] += jnp.sum(acc * acc, axis=0, keepdims=True)


def head_product(joined, value):
    rows, depth = joined.shape
    width, slab = depth // Z, value.shape[1]
    out, squares = pl.pallas_call(
        head_kernel,
        grid=(Z,),
        in_specs=[
            pl.BlockSpec((rows, width), lambda i: (0, i)),
            pl.BlockSpec(value.shape, lambda i: (0, 0)),
        ],
        out_specs=[
            pl.BlockSpec((1, width, slab), lambda i: (i, 0, 0)),
            pl.BlockSpec((1, slab), lambda i: (0, 0)),
        ],
        out_shape=[
            jax.ShapeDtypeStruct((Z, width, slab), jnp.float32),
            jax.ShapeDtypeStruct((1, slab), jnp.float32),
        ],
        compiler_params=kernel_params(),
        cost_estimate=pl.CostEstimate(
            flops=2 * rows * depth * slab, bytes_accessed=7 * 2**20, transcendentals=0
        ),
    )(joined, value)
    return out, squares


def scale_kernel(scale_ref, fc_ref, head_ref, fc_out_ref, head_out_ref):
    scale = scale_ref[0, 0]
    slab = head_ref.shape[3]
    fc_out_ref[...] = fc_ref[...] * scale
    for side in range(ZH):
        head_out_ref[:, side * slab : (side + 1) * slab] = head_ref[side, 0] * scale


def scaled(fc_grad, head_grad, scale):
    deep, width = fc_grad.shape
    _, _, rows, slab = head_grad.shape
    return pl.pallas_call(
        scale_kernel,
        grid=(ZL,),
        in_specs=[
            pl.BlockSpec(memory_space=pltpu.SMEM),
            pl.BlockSpec((deep // ZL, width), lambda i: (i, 0)),
            pl.BlockSpec((ZH, 1, rows, slab), lambda i: (0, i, 0, 0)),
        ],
        out_specs=[
            pl.BlockSpec((deep // ZL, width), lambda i: (i, 0)),
            pl.BlockSpec((rows, ZH * slab), lambda i: (0, i)),
        ],
        out_shape=[
            jax.ShapeDtypeStruct(fc_grad.shape, jnp.float32),
            jax.ShapeDtypeStruct((rows, Z * slab), jnp.float32),
        ],
        compiler_params=kernel_params(),
        cost_estimate=pl.CostEstimate(
            flops=fc_grad.size + head_grad.size,
            bytes_accessed=8 * (fc_grad.size + head_grad.size),
            transcendentals=0,
        ),
    )(scale.reshape(1, 1), fc_grad, head_grad)


def total(value):
    value = value + swap(value)
    for axis in ("x", "y"):
        value = (value + shift(value, axis, 2)) + (shift(value, axis, 1) + shift(value, axis, -1))
    parts = [value]
    for by in range(1, Z):
        parts.append(lax.ppermute(value, DEPTH, [(i, i ^ by) for i in range(Z)]))
    while len(parts) > 1:
        parts = [first + second for first, second in zip(parts[::2], parts[1::2])]
    return parts[0]


def per_device(
    hidden_rows, fc_weight, head_weight, target_probs, token_ids, vocab_map, segment_ids, loss_mask
):
    x, core, y = lax.axis_index("x"), lax.axis_index("core"), lax.axis_index("y")
    zh, zl = lax.axis_index("zh"), lax.axis_index("zl")
    rows = hidden_rows.shape[1]
    tokens = rows * Y * ZH
    low = rows // X
    width = fc_weight.shape[2]
    depth = width * Z
    slab = head_weight.shape[1] // Z
    columns = slab * X
    same_side = core == zh

    flat = hidden_rows.transpose(1, 0, 2).reshape(rows, -1)
    far = lax.ppermute(flat, "zh", [(0, 1), (1, 0)])
    rows_near = lax.all_gather(flat, "y", axis=0, tiled=True)
    rows_far = lax.all_gather(far, "y", axis=0, tiled=True)

    head = head_weight.reshape(width, ZL, ZH, slab).transpose(2, 1, 0, 3).reshape(Z, width, slab)
    head, _ = lax.optimization_barrier((head, far))
    head = lax.all_to_all(head, DEPTH, 0, 0).reshape(depth, slab)

    targets = target_probs.reshape(X, low, ZH, slab).transpose(0, 2, 1, 3)
    targets = targets.reshape(X * ZH, low, slab)
    targets, head = lax.optimization_barrier((targets, head))
    targets = lax.all_to_all(targets, ("x", "zh"), 0, 0).reshape(X, ZH, low, slab)

    head = lax.all_gather(head, "x", axis=1, tiled=True)
    fc_flat = fc_weight.reshape(-1, width)

    part_near = jnp.dot(rows_near, fc_flat, preferred_element_type=jnp.float32)
    part_near, targets = lax.optimization_barrier((part_near, targets))
    part_far = jnp.dot(rows_far, fc_flat, preferred_element_type=jnp.float32)
    theirs = swap(jnp.where(same_side, part_far, part_near))
    partial = jnp.where(same_side, part_near, part_far) + theirs
    partial = partial.reshape(Y, X, low, width)
    joined_own = pick(partial, x, 1)
    for by in (1, -1, 2):
        joined_own = joined_own + shift(pick(partial, (x + by) % X, 1), "x", by)
    joined_own = joined_own.reshape(Y * low, width).astype(jnp.bfloat16)
    joined_wide = spread(joined_own, DEPTH, Z).transpose(1, 0, 2).reshape(Y * low, depth)
    mine, theirs = joined_wide.reshape(Y, low, depth), swap(joined_wide).reshape(Y, low, depth)
    joined_all = lax.all_gather(joined_wide, ("x", "core"), axis=0, tiled=True)
    joined_pair = jnp.stack(
        [jnp.where(core == 0, mine, theirs), jnp.where(core == 0, theirs, mine)], axis=1
    )

    partial = jnp.dot(
        joined_pair.reshape(Y * ZH * low, depth), head, preferred_element_type=jnp.float32
    )
    partial = partial.reshape(Y, ZH * low, columns)
    logits = pick(partial, y, 0)
    for by in (1, -1, 2):
        logits = logits + shift(pick(partial, (y + by) % Y, 0), "y", by)

    next_segment = jnp.concatenate([segment_ids[1:], jnp.full((1,), -1, jnp.int32)])
    kept_all = loss_mask * (segment_ids == next_segment).astype(jnp.int32)
    kept_count = jnp.maximum(jnp.sum(kept_all), 1).astype(jnp.float32)

    def own(value):
        value = pick(value.reshape(Y, ZH, X, low), y, 0)
        return pick(value, x, 1).reshape(ZH * low)

    kept_tokens = own(kept_all).astype(jnp.float32)
    labels = vocab_map[own(token_ids)]
    lane = jnp.arange(columns, dtype=jnp.int32)
    vocab_id = (((lane // slab * C + core) * ZL + zl) * ZH + zh) * slab + lane % slab
    onehot = (labels[:, None] == vocab_id[None, :]).astype(jnp.float32)

    targets = targets.transpose(1, 2, 0, 3).reshape(ZH * low, columns).astype(jnp.float32)
    local_max = jnp.max(logits, axis=1)
    local_total = jnp.sum(jnp.exp(logits - local_max[:, None]), axis=1)
    picked = jnp.sum(onehot * logits, axis=1)
    dotted = jnp.sum(targets * logits, axis=1)
    prob_mass = jnp.sum(targets, axis=1)
    stats = jnp.stack([local_max, local_total, dotted, prob_mass, picked])
    stats = spread(stats, ("core", "zh", "zl"), C * Z)
    row_peak = jnp.max(stats[:, 0], axis=0)
    exp_total = jnp.sum(stats[:, 1] * jnp.exp(stats[:, 0] - row_peak), axis=0)
    dotted, prob_mass, picked = jnp.sum(stats[:, 2:], axis=0)
    log_total = row_peak + jnp.log(exp_total)
    token_loss = kept_tokens * (log_total * prob_mass - dotted + log_total - picked)
    loss_part = jnp.sum(token_loss) / kept_count / (C * Z)
    draft_probs = jnp.exp(logits - log_total[:, None])
    dlogits = (
        kept_tokens[:, None] * (draft_probs * (prob_mass[:, None] + 1.0) - targets - onehot)
    ).astype(jnp.bfloat16)

    shard = [(y, dlogits)] + [((y - by) % Y, shift(dlogits, "y", by)) for by in (1, -1, 2)]
    shard = arrange(shard).reshape(Y, ZH, low, columns)
    shard, joined_all = lax.optimization_barrier((shard, joined_all))

    def feature(side):
        side = pick(shard, side, 1).reshape(Y * low, columns)
        return lax.dot_general(side, head, (((1,), (1,)), ((), ())), preferred_element_type=jnp.float32)

    theirs = swap(feature(1 - core))
    feature_part = feature(core) + theirs
    feature_part = lax.all_to_all(feature_part.reshape(Y * low, Z, width), DEPTH, 1, 0)

    dlogits_all = lax.all_gather(shard.reshape(-1, columns), "x", axis=0, tiled=True)
    dlogits_all = lax.dynamic_slice_in_dim(dlogits_all, x * slab, slab, 1)
    dlogits_all = dlogits_all.reshape(X, Y, ZH, low, slab).transpose(0, 2, 1, 3, 4)
    head_grad, head_squares = head_product(joined_all, dlogits_all.reshape(tokens, slab))
    feature_part, head_grad = lax.optimization_barrier((feature_part, head_grad))
    head_grad = lax.all_to_all(head_grad, DEPTH, 0, 0)

    feature_own = jnp.sum(feature_part, axis=0).astype(jnp.bfloat16)

    ring = [(x, feature_own)]
    ring += [((x - by) % X, shift(feature_own, "x", by)) for by in (1, -1, 2)]
    ring = arrange(ring).reshape(X, Y, low, width).transpose(1, 0, 2, 3)
    other = swap(ring)
    feature_all = jnp.stack([jnp.where(same_side, ring, other), jnp.where(same_side, other, ring)])
    fc_grad, fc_squares = fc_product([rows_near, rows_far], feature_all.reshape(tokens, width))

    loss_lane = jnp.where(jnp.arange(width) == 0, loss_part, 0.0)[None, :]
    sums = total(jnp.concatenate([head_squares + fc_squares, loss_lane]))
    sums = jnp.sum(sums, axis=1)
    entries = 3.0 * D * D + 1.0 * D * VD
    scale = lax.rsqrt(sums[0] / entries + 1e-06)
    fc_step, head_step = scaled(fc_grad, head_grad.reshape(ZH, ZL, width, slab), scale)
    return (fc_step.reshape(fc_weight.shape), head_step, sums[1])


def solution(mesh):
    fine = Mesh(mesh.devices.reshape(X, C, Y, ZH, ZL), ("x", "core", "y", "zh", "zl"))
    tgt, dp, vocab = ("x", "core"), ("y", "zh"), ("zl",)
    in_specs = (
        P(None, dp, tgt),
        P(None, tgt, dp + vocab),
        P(dp + vocab, tgt),
        P(dp, tgt + vocab),
        P(),
        P(),
        P(),
        P(),
    )
    out_specs = (P(None, tgt, dp + vocab), P(dp + vocab, tgt), P())
    return jax.shard_map(
        per_device, mesh=fine, in_specs=in_specs, out_specs=out_specs, check_vma=False
    )
```

```python
import jax
import jax.numpy as jnp
from jax import lax
from jax.experimental import pallas as pl
from jax.experimental.pallas import tpu as pltpu
from jax.sharding import Mesh, PartitionSpec as P

D = 8192
VD = 16384
X, C, Y, ZH, ZL = 4, 2, 4, 2, 4
Z = ZH * ZL
DEPTH = ("zh", "zl")


def spread(value, axes, count):
    return lax.all_to_all(jnp.broadcast_to(value[None], (count,) + value.shape), axes, 0, 0)


def swap(value):
    return lax.ppermute(value, "core", [(0, 1), (1, 0)])


def shift(value, axis, by):
    return lax.ppermute(value, axis, [(i, (i + by) % 4) for i in range(4)])


def pick(value, index, axis):
    return lax.dynamic_index_in_dim(value, index, axis, keepdims=False)


def arrange(parts):
    out = jnp.zeros((len(parts),) + parts[0][1].shape, parts[0][1].dtype)
    for index, part in parts:
        out = lax.dynamic_update_index_in_dim(out, part, index, 0)
    return out


VMEM_BYTES = 56 * 1024 * 1024


def kernel_params():
    return pltpu.CompilerParams(
        dimension_semantics=("arbitrary",), vmem_limit_bytes=VMEM_BYTES
    )


def fc_kernel(*refs):
    row_refs, (feature_ref, out_ref, squares_ref) = refs[:-3], refs[-3:]
    row = 0
    acc = None
    for ref in row_refs:
        rows = ref.shape[0]
        term = lax.dot_general(
            ref[...],
            feature_ref[row : row + rows, :],
            (((0,), (0,)), ((), ())),
            preferred_element_type=jnp.float32,
        )
        acc = term if acc is None else acc + term
        row += rows
    out_ref[...] = acc

    @pl.when(pl.program_id(0) == 0)
    def _():
        squares_ref[...] = jnp.zeros_like(squares_ref)

    squares_ref[...] += jnp.sum(acc * acc, axis=0, keepdims=True)


def fc_product(groups, feature):
    block = 512
    deep, width = groups[0].shape[1], feature.shape[1]
    out, squares = pl.pallas_call(
        fc_kernel,
        grid=(deep // block,),
        in_specs=[
            pl.BlockSpec((part.shape[0] // 2, block), lambda i, half=half: (half, i))
            for part in groups
            for half in range(2)
        ]
        + [pl.BlockSpec(feature.shape, lambda i: (0, 0))],
        out_specs=[
            pl.BlockSpec((block, width), lambda i: (i, 0)),
            pl.BlockSpec((1, width), lambda i: (0, 0)),
        ],
        out_shape=[
            jax.ShapeDtypeStruct((deep, width), jnp.float32),
            jax.ShapeDtypeStruct((1, width), jnp.float32),
        ],
        compiler_params=kernel_params(),
        cost_estimate=pl.CostEstimate(
            flops=2 * feature.shape[0] * deep * width, bytes_accessed=10 * 2**20, transcendentals=0
        ),
    )(*[part for part in groups for _ in range(2)], feature)
    return out, squares


def head_kernel(joined_ref, value_ref, out_ref, squares_ref):
    acc = lax.dot_general(
        joined_ref[...],
        value_ref[...],
        (((0,), (0,)), ((), ())),
        preferred_element_type=jnp.float32,
    )
    out_ref[0] = acc

    @pl.when(pl.program_id(0) == 0)
    def _():
        squares_ref[...] = jnp.zeros_like(squares_ref)

    squares_ref[...] += jnp.sum(acc * acc, axis=0, keepdims=True)


def head_product(joined, value):
    rows, depth = joined.shape
    width, slab = depth // Z, value.shape[1]
    out, squares = pl.pallas_call(
        head_kernel,
        grid=(Z,),
        in_specs=[
            pl.BlockSpec((rows, width), lambda i: (0, i)),
            pl.BlockSpec(value.shape, lambda i: (0, 0)),
        ],
        out_specs=[
            pl.BlockSpec((1, width, slab), lambda i: (i, 0, 0)),
            pl.BlockSpec((1, slab), lambda i: (0, 0)),
        ],
        out_shape=[
            jax.ShapeDtypeStruct((Z, width, slab), jnp.float32),
            jax.ShapeDtypeStruct((1, slab), jnp.float32),
        ],
        compiler_params=kernel_params(),
        cost_estimate=pl.CostEstimate(
            flops=2 * rows * depth * slab, bytes_accessed=7 * 2**20, transcendentals=0
        ),
    )(joined, value)
    return out, squares


def scale_kernel(scale_ref, fc_ref, head_ref, fc_out_ref, head_out_ref):
    scale = scale_ref[0, 0]
    slab = head_ref.shape[3]
    fc_out_ref[...] = fc_ref[...] * scale
    for side in range(ZH):
        head_out_ref[:, side * slab : (side + 1) * slab] = head_ref[side, 0] * scale


def scaled(fc_grad, head_grad, scale):
    deep, width = fc_grad.shape
    _, _, rows, slab = head_grad.shape
    return pl.pallas_call(
        scale_kernel,
        grid=(ZL,),
        in_specs=[
            pl.BlockSpec(memory_space=pltpu.SMEM),
            pl.BlockSpec((deep // ZL, width), lambda i: (i, 0)),
            pl.BlockSpec((ZH, 1, rows, slab), lambda i: (0, i, 0, 0)),
        ],
        out_specs=[
            pl.BlockSpec((deep // ZL, width), lambda i: (i, 0)),
            pl.BlockSpec((rows, ZH * slab), lambda i: (0, i)),
        ],
        out_shape=[
            jax.ShapeDtypeStruct(fc_grad.shape, jnp.float32),
            jax.ShapeDtypeStruct((rows, Z * slab), jnp.float32),
        ],
        compiler_params=kernel_params(),
        cost_estimate=pl.CostEstimate(
            flops=fc_grad.size + head_grad.size,
            bytes_accessed=8 * (fc_grad.size + head_grad.size),
            transcendentals=0,
        ),
    )(scale.reshape(1, 1), fc_grad, head_grad)


def total(value):
    value = value + swap(value)
    for axis in ("x", "y"):
        value = (value + shift(value, axis, 2)) + (shift(value, axis, 1) + shift(value, axis, -1))
    at = [lax.ppermute(value, DEPTH, [(i, i ^ by) for i in range(Z)]) for by in (1, 2, 3)]
    value = (value + at[0]) + (at[1] + at[2])
    return value + lax.ppermute(value, DEPTH, [(i, i ^ ZL) for i in range(Z)])


def per_device(
    hidden_rows, fc_weight, head_weight, target_probs, token_ids, vocab_map, segment_ids, loss_mask
):
    x, core, y = lax.axis_index("x"), lax.axis_index("core"), lax.axis_index("y")
    zh, zl = lax.axis_index("zh"), lax.axis_index("zl")
    rows = hidden_rows.shape[1]
    tokens = rows * Y * ZH
    low = rows // X
    width = fc_weight.shape[2]
    depth = width * Z
    slab = head_weight.shape[1] // Z
    columns = slab * X
    same_side = core == zh

    flat = hidden_rows.transpose(1, 0, 2).reshape(rows, -1)
    far = lax.ppermute(flat, "zh", [(0, 1), (1, 0)])
    rows_near = lax.all_gather(flat, "y", axis=0, tiled=True)
    rows_far = lax.all_gather(far, "y", axis=0, tiled=True)

    head = head_weight.reshape(width, ZL, ZH, slab).transpose(2, 1, 0, 3).reshape(Z, width, slab)
    head, _ = lax.optimization_barrier((head, far))
    head = lax.all_to_all(head, DEPTH, 0, 0).reshape(depth, slab)

    targets = target_probs.reshape(X, low, ZH, slab).transpose(0, 2, 1, 3)
    targets = targets.reshape(X * ZH, low, slab)
    targets, head = lax.optimization_barrier((targets, head))
    targets = lax.all_to_all(targets, ("x", "zh"), 0, 0).reshape(X, ZH, low, slab)

    head = lax.all_gather(head, "x", axis=1, tiled=True)
    fc_flat = fc_weight.reshape(-1, width)

    part_near = jnp.dot(rows_near, fc_flat, preferred_element_type=jnp.float32)
    part_near, targets = lax.optimization_barrier((part_near, targets))
    part_far = jnp.dot(rows_far, fc_flat, preferred_element_type=jnp.float32)
    theirs = swap(jnp.where(same_side, part_far, part_near))
    partial = jnp.where(same_side, part_near, part_far) + theirs
    partial = partial.reshape(Y, X, low, width)
    joined_own = pick(partial, x, 1)
    for by in (1, -1, 2):
        joined_own = joined_own + shift(pick(partial, (x + by) % X, 1), "x", by)
    joined_own = joined_own.reshape(Y * low, width).astype(jnp.bfloat16)
    joined_wide = spread(joined_own, DEPTH, Z).transpose(1, 0, 2).reshape(Y * low, depth)
    mine, theirs = joined_wide.reshape(Y, low, depth), swap(joined_wide).reshape(Y, low, depth)
    joined_all = lax.all_gather(joined_wide, ("x", "core"), axis=0, tiled=True)
    joined_pair = jnp.stack(
        [jnp.where(core == 0, mine, theirs), jnp.where(core == 0, theirs, mine)], axis=1
    )

    partial = jnp.dot(
        joined_pair.reshape(Y * ZH * low, depth), head, preferred_element_type=jnp.float32
    )
    partial = partial.reshape(Y, ZH * low, columns)
    logits = pick(partial, y, 0)
    for by in (1, -1, 2):
        logits = logits + shift(pick(partial, (y + by) % Y, 0), "y", by)

    next_segment = jnp.concatenate([segment_ids[1:], jnp.full((1,), -1, jnp.int32)])
    kept_all = loss_mask * (segment_ids == next_segment).astype(jnp.int32)
    kept_count = jnp.maximum(jnp.sum(kept_all), 1).astype(jnp.float32)

    def own(value):
        value = pick(value.reshape(Y, ZH, X, low), y, 0)
        return pick(value, x, 1).reshape(ZH * low)

    kept_tokens = own(kept_all).astype(jnp.float32)
    labels = vocab_map[own(token_ids)]
    lane = jnp.arange(columns, dtype=jnp.int32)
    vocab_id = (((lane // slab * C + core) * ZL + zl) * ZH + zh) * slab + lane % slab
    onehot = (labels[:, None] == vocab_id[None, :]).astype(jnp.float32)

    targets = targets.transpose(1, 2, 0, 3).reshape(ZH * low, columns).astype(jnp.float32)
    local_max = jnp.max(logits, axis=1)
    local_total = jnp.sum(jnp.exp(logits - local_max[:, None]), axis=1)
    picked = jnp.sum(onehot * logits, axis=1)
    dotted = jnp.sum(targets * logits, axis=1)
    prob_mass = jnp.sum(targets, axis=1)
    stats = jnp.stack([local_max, local_total, dotted, prob_mass, picked])
    stats = spread(stats, ("core", "zh", "zl"), C * Z)
    row_peak = jnp.max(stats[:, 0], axis=0)
    exp_total = jnp.sum(stats[:, 1] * jnp.exp(stats[:, 0] - row_peak), axis=0)
    dotted, prob_mass, picked = jnp.sum(stats[:, 2:], axis=0)
    log_total = row_peak + jnp.log(exp_total)
    token_loss = kept_tokens * (log_total * prob_mass - dotted + log_total - picked)
    loss_part = jnp.sum(token_loss) / kept_count / (C * Z)
    draft_probs = jnp.exp(logits - log_total[:, None])
    dlogits = (
        kept_tokens[:, None] * (draft_probs * (prob_mass[:, None] + 1.0) - targets - onehot)
    ).astype(jnp.bfloat16)

    shard = [(y, dlogits)] + [((y - by) % Y, shift(dlogits, "y", by)) for by in (1, -1, 2)]
    shard = arrange(shard).reshape(Y, ZH, low, columns)
    shard, joined_all = lax.optimization_barrier((shard, joined_all))

    def feature(side):
        side = pick(shard, side, 1).reshape(Y * low, columns)
        return lax.dot_general(side, head, (((1,), (1,)), ((), ())), preferred_element_type=jnp.float32)

    theirs = swap(feature(1 - core))
    feature_part = feature(core) + theirs
    feature_part = lax.all_to_all(feature_part.reshape(Y * low, Z, width), DEPTH, 1, 0)

    dlogits_all = lax.all_gather(shard.reshape(-1, columns), "x", axis=0, tiled=True)
    dlogits_all = lax.dynamic_slice_in_dim(dlogits_all, x * slab, slab, 1)
    dlogits_all = dlogits_all.reshape(X, Y, ZH, low, slab).transpose(0, 2, 1, 3, 4)
    head_grad, head_squares = head_product(joined_all, dlogits_all.reshape(tokens, slab))
    feature_part, head_grad = lax.optimization_barrier((feature_part, head_grad))
    head_grad = lax.all_to_all(head_grad, DEPTH, 0, 0)

    feature_own = jnp.sum(feature_part, axis=0).astype(jnp.bfloat16)

    ring = [(x, feature_own)]
    ring += [((x - by) % X, shift(feature_own, "x", by)) for by in (1, -1, 2)]
    ring = arrange(ring).reshape(X, Y, low, width).transpose(1, 0, 2, 3)
    other = swap(ring)
    feature_all = jnp.stack([jnp.where(same_side, ring, other), jnp.where(same_side, other, ring)])
    fc_grad, fc_squares = fc_product([rows_near, rows_far], feature_all.reshape(tokens, width))

    loss_lane = jnp.where(jnp.arange(width) == 0, loss_part, 0.0)[None, :]
    sums = total(jnp.concatenate([head_squares + fc_squares, loss_lane]))
    sums = jnp.sum(sums, axis=1)
    entries = 3.0 * D * D + 1.0 * D * VD
    scale = lax.rsqrt(sums[0] / entries + 1e-06)
    fc_step, head_step = scaled(fc_grad, head_grad.reshape(ZH, ZL, width, slab), scale)
    return (fc_step.reshape(fc_weight.shape), head_step, sums[1])


def solution(mesh):
    fine = Mesh(mesh.devices.reshape(X, C, Y, ZH, ZL), ("x", "core", "y", "zh", "zl"))
    tgt, dp, vocab = ("x", "core"), ("y", "zh"), ("zl",)
    in_specs = (
        P(None, dp, tgt),
        P(None, tgt, dp + vocab),
        P(dp + vocab, tgt),
        P(dp, tgt + vocab),
        P(),
        P(),
        P(),
        P(),
    )
    out_specs = (P(None, tgt, dp + vocab), P(dp + vocab, tgt), P())
    return jax.shard_map(
        per_device, mesh=fine, in_specs=in_specs, out_specs=out_specs, check_vma=False
    )
```

```python
import jax
import jax.numpy as jnp
from jax import lax
from jax.experimental import pallas as pl
from jax.experimental.pallas import tpu as pltpu
from jax.sharding import Mesh, PartitionSpec as P

D = 8192
VD = 16384
X, C, Y, ZH, ZL = 4, 2, 4, 2, 4
Z = ZH * ZL
DEPTH = ("zh", "zl")


def spread(value, axes, count):
    return lax.all_to_all(jnp.broadcast_to(value[None], (count,) + value.shape), axes, 0, 0)


def swap(value):
    return lax.ppermute(value, "core", [(0, 1), (1, 0)])


def shift(value, axis, by):
    return lax.ppermute(value, axis, [(i, (i + by) % 4) for i in range(4)])


def pick(value, index, axis):
    return lax.dynamic_index_in_dim(value, index, axis, keepdims=False)


def arrange(parts):
    out = jnp.zeros((len(parts),) + parts[0][1].shape, parts[0][1].dtype)
    for index, part in parts:
        out = lax.dynamic_update_index_in_dim(out, part, index, 0)
    return out


VMEM_BYTES = 56 * 1024 * 1024


def kernel_params(vmem_bytes=VMEM_BYTES):
    return pltpu.CompilerParams(
        dimension_semantics=("arbitrary",), vmem_limit_bytes=vmem_bytes
    )


def fc_kernel(*refs):
    row_refs, (feature_ref, out_ref, squares_ref) = refs[:-3], refs[-3:]
    row = 0
    acc = None
    for ref in row_refs:
        rows = ref.shape[0]
        term = lax.dot_general(
            ref[...],
            feature_ref[row : row + rows, :],
            (((0,), (0,)), ((), ())),
            preferred_element_type=jnp.float32,
        )
        acc = term if acc is None else acc + term
        row += rows
    out_ref[...] = acc

    @pl.when(pl.program_id(0) == 0)
    def _():
        squares_ref[...] = jnp.zeros_like(squares_ref)

    squares_ref[...] += jnp.sum(acc * acc, axis=0, keepdims=True)


def fc_product(groups, feature):
    block = 512
    deep, width = groups[0].shape[1], feature.shape[1]
    out, squares = pl.pallas_call(
        fc_kernel,
        grid=(deep // block,),
        in_specs=[
            pl.BlockSpec((part.shape[0] // 2, block), lambda i, half=half: (half, i))
            for part in groups
            for half in range(2)
        ]
        + [pl.BlockSpec(feature.shape, lambda i: (0, 0))],
        out_specs=[
            pl.BlockSpec((block, width), lambda i: (i, 0)),
            pl.BlockSpec((1, width), lambda i: (0, 0)),
        ],
        out_shape=[
            jax.ShapeDtypeStruct((deep, width), jnp.float32),
            jax.ShapeDtypeStruct((1, width), jnp.float32),
        ],
        compiler_params=kernel_params(24 * 1024 * 1024),
        cost_estimate=pl.CostEstimate(
            flops=2 * feature.shape[0] * deep * width, bytes_accessed=10 * 2**20, transcendentals=0
        ),
    )(*[part for part in groups for _ in range(2)], feature)
    return out, squares


def head_kernel(joined_ref, value_ref, out_ref, squares_ref):
    acc = lax.dot_general(
        joined_ref[...],
        value_ref[...],
        (((0,), (0,)), ((), ())),
        preferred_element_type=jnp.float32,
    )
    out_ref[0] = acc

    @pl.when(pl.program_id(0) == 0)
    def _():
        squares_ref[...] = jnp.zeros_like(squares_ref)

    squares_ref[...] += jnp.sum(acc * acc, axis=0, keepdims=True)


def head_product(joined, value):
    rows, depth = joined.shape
    width, slab = depth // Z, value.shape[1]
    out, squares = pl.pallas_call(
        head_kernel,
        grid=(Z,),
        in_specs=[
            pl.BlockSpec((rows, width), lambda i: (0, i)),
            pl.BlockSpec(value.shape, lambda i: (0, 0)),
        ],
        out_specs=[
            pl.BlockSpec((1, width, slab), lambda i: (i, 0, 0)),
            pl.BlockSpec((1, slab), lambda i: (0, 0)),
        ],
        out_shape=[
            jax.ShapeDtypeStruct((Z, width, slab), jnp.float32),
            jax.ShapeDtypeStruct((1, slab), jnp.float32),
        ],
        compiler_params=kernel_params(),
        cost_estimate=pl.CostEstimate(
            flops=2 * rows * depth * slab, bytes_accessed=7 * 2**20, transcendentals=0
        ),
    )(joined, value)
    return out, squares


def scale_kernel(scale_ref, fc_ref, head_ref, fc_out_ref, head_out_ref):
    scale = scale_ref[0, 0]
    slab = head_ref.shape[3]
    fc_out_ref[...] = fc_ref[...] * scale
    for side in range(ZH):
        head_out_ref[:, side * slab : (side + 1) * slab] = head_ref[side, 0] * scale


def scaled(fc_grad, head_grad, scale):
    deep, width = fc_grad.shape
    _, _, rows, slab = head_grad.shape
    return pl.pallas_call(
        scale_kernel,
        grid=(ZL,),
        in_specs=[
            pl.BlockSpec(memory_space=pltpu.SMEM),
            pl.BlockSpec((deep // ZL, width), lambda i: (i, 0)),
            pl.BlockSpec((ZH, 1, rows, slab), lambda i: (0, i, 0, 0)),
        ],
        out_specs=[
            pl.BlockSpec((deep // ZL, width), lambda i: (i, 0)),
            pl.BlockSpec((rows, ZH * slab), lambda i: (0, i)),
        ],
        out_shape=[
            jax.ShapeDtypeStruct(fc_grad.shape, jnp.float32),
            jax.ShapeDtypeStruct((rows, Z * slab), jnp.float32),
        ],
        compiler_params=kernel_params(),
        cost_estimate=pl.CostEstimate(
            flops=fc_grad.size + head_grad.size,
            bytes_accessed=8 * (fc_grad.size + head_grad.size),
            transcendentals=0,
        ),
    )(scale.reshape(1, 1), fc_grad, head_grad)


def total(value):
    value = value + swap(value)
    for axis in ("x", "y"):
        value = (value + shift(value, axis, 2)) + (shift(value, axis, 1) + shift(value, axis, -1))
    at = [lax.ppermute(value, DEPTH, [(i, i ^ by) for i in range(Z)]) for by in (1, 2, 3)]
    value = (value + at[0]) + (at[1] + at[2])
    return value + lax.ppermute(value, DEPTH, [(i, i ^ ZL) for i in range(Z)])


def per_device(
    hidden_rows, fc_weight, head_weight, target_probs, token_ids, vocab_map, segment_ids, loss_mask
):
    x, core, y = lax.axis_index("x"), lax.axis_index("core"), lax.axis_index("y")
    zh, zl = lax.axis_index("zh"), lax.axis_index("zl")
    rows = hidden_rows.shape[1]
    tokens = rows * Y * ZH
    low = rows // X
    width = fc_weight.shape[2]
    depth = width * Z
    slab = head_weight.shape[1] // Z
    columns = slab * X
    same_side = core == zh

    flat = hidden_rows.transpose(1, 0, 2).reshape(rows, -1)
    far = lax.ppermute(flat, "zh", [(0, 1), (1, 0)])
    rows_near = lax.all_gather(flat, "y", axis=0, tiled=True)
    rows_far = lax.all_gather(far, "y", axis=0, tiled=True)

    head = head_weight.reshape(width, ZL, ZH, slab).transpose(2, 1, 0, 3).reshape(Z, width, slab)
    head, _ = lax.optimization_barrier((head, far))
    head = lax.all_to_all(head, DEPTH, 0, 0).reshape(depth, slab)

    targets = target_probs.reshape(X, low, ZH, slab).transpose(0, 2, 1, 3)
    targets = targets.reshape(X * ZH, low, slab)
    targets, head = lax.optimization_barrier((targets, head))
    targets = lax.all_to_all(targets, ("x", "zh"), 0, 0).reshape(X, ZH, low, slab)

    head = lax.all_gather(head, "x", axis=1, tiled=True)
    fc_flat = fc_weight.reshape(-1, width)

    part_near = jnp.dot(rows_near, fc_flat, preferred_element_type=jnp.float32)
    part_near, targets = lax.optimization_barrier((part_near, targets))
    part_far = jnp.dot(rows_far, fc_flat, preferred_element_type=jnp.float32)
    theirs = swap(jnp.where(same_side, part_far, part_near))
    partial = jnp.where(same_side, part_near, part_far) + theirs
    partial = partial.reshape(Y, X, low, width)
    joined_own = pick(partial, x, 1)
    for by in (1, -1, 2):
        joined_own = joined_own + shift(pick(partial, (x + by) % X, 1), "x", by)
    joined_own = joined_own.reshape(Y * low, width).astype(jnp.bfloat16)
    joined_wide = spread(joined_own, DEPTH, Z).transpose(1, 0, 2).reshape(Y * low, depth)
    mine, theirs = joined_wide.reshape(Y, low, depth), swap(joined_wide).reshape(Y, low, depth)
    joined_all = lax.all_gather(joined_wide, ("x", "core"), axis=0, tiled=True)
    joined_pair = jnp.stack(
        [jnp.where(core == 0, mine, theirs), jnp.where(core == 0, theirs, mine)], axis=1
    )

    partial = jnp.dot(
        joined_pair.reshape(Y * ZH * low, depth), head, preferred_element_type=jnp.float32
    )
    partial = partial.reshape(Y, ZH * low, columns)
    logits = pick(partial, y, 0)
    for by in (1, -1, 2):
        logits = logits + shift(pick(partial, (y + by) % Y, 0), "y", by)

    next_segment = jnp.concatenate([segment_ids[1:], jnp.full((1,), -1, jnp.int32)])
    kept_all = loss_mask * (segment_ids == next_segment).astype(jnp.int32)
    kept_count = jnp.maximum(jnp.sum(kept_all), 1).astype(jnp.float32)

    def own(value):
        value = pick(value.reshape(Y, ZH, X, low), y, 0)
        return pick(value, x, 1).reshape(ZH * low)

    kept_tokens = own(kept_all).astype(jnp.float32)
    labels = vocab_map[own(token_ids)]
    lane = jnp.arange(columns, dtype=jnp.int32)
    vocab_id = (((lane // slab * C + core) * ZL + zl) * ZH + zh) * slab + lane % slab
    onehot = (labels[:, None] == vocab_id[None, :]).astype(jnp.float32)

    targets = targets.transpose(1, 2, 0, 3).reshape(ZH * low, columns).astype(jnp.float32)
    local_max = jnp.max(logits, axis=1)
    local_total = jnp.sum(jnp.exp(logits - local_max[:, None]), axis=1)
    picked = jnp.sum(onehot * logits, axis=1)
    dotted = jnp.sum(targets * logits, axis=1)
    prob_mass = jnp.sum(targets, axis=1)
    stats = jnp.stack([local_max, local_total, dotted, prob_mass, picked])
    stats = spread(stats, ("core", "zh", "zl"), C * Z)
    row_peak = jnp.max(stats[:, 0], axis=0)
    exp_total = jnp.sum(stats[:, 1] * jnp.exp(stats[:, 0] - row_peak), axis=0)
    dotted, prob_mass, picked = jnp.sum(stats[:, 2:], axis=0)
    log_total = row_peak + jnp.log(exp_total)
    token_loss = kept_tokens * (log_total * prob_mass - dotted + log_total - picked)
    loss_part = jnp.sum(token_loss) / kept_count / (C * Z)
    draft_probs = jnp.exp(logits - log_total[:, None])
    dlogits = (
        kept_tokens[:, None] * (draft_probs * (prob_mass[:, None] + 1.0) - targets - onehot)
    ).astype(jnp.bfloat16)

    shard = [(y, dlogits)] + [((y - by) % Y, shift(dlogits, "y", by)) for by in (1, -1, 2)]
    shard = arrange(shard).reshape(Y, ZH, low, columns)
    shard, joined_all = lax.optimization_barrier((shard, joined_all))

    def feature(side):
        side = pick(shard, side, 1).reshape(Y * low, columns)
        return lax.dot_general(side, head, (((1,), (1,)), ((), ())), preferred_element_type=jnp.float32)

    theirs = swap(feature(1 - core))
    feature_part = feature(core) + theirs
    feature_part = lax.all_to_all(feature_part.reshape(Y * low, Z, width), DEPTH, 1, 0)

    dlogits_all = lax.all_gather(shard.reshape(-1, columns), "x", axis=0, tiled=True)
    dlogits_all = lax.dynamic_slice_in_dim(dlogits_all, x * slab, slab, 1)
    dlogits_all = dlogits_all.reshape(X, Y, ZH, low, slab).transpose(0, 2, 1, 3, 4)
    head_grad, head_squares = head_product(joined_all, dlogits_all.reshape(tokens, slab))
    feature_part, head_grad = lax.optimization_barrier((feature_part, head_grad))
    head_grad = lax.all_to_all(head_grad, DEPTH, 0, 0)

    feature_own = jnp.sum(feature_part, axis=0).astype(jnp.bfloat16)

    ring = [(x, feature_own)]
    ring += [((x - by) % X, shift(feature_own, "x", by)) for by in (1, -1, 2)]
    ring = arrange(ring).reshape(X, Y, low, width).transpose(1, 0, 2, 3)
    other = swap(ring)
    feature_all = jnp.stack([jnp.where(same_side, ring, other), jnp.where(same_side, other, ring)])
    fc_grad, fc_squares = fc_product([rows_near, rows_far], feature_all.reshape(tokens, width))

    loss_lane = jnp.where(jnp.arange(width) == 0, loss_part, 0.0)[None, :]
    sums = total(jnp.concatenate([head_squares + fc_squares, loss_lane]))
    sums = jnp.sum(sums, axis=1)
    entries = 3.0 * D * D + 1.0 * D * VD
    scale = lax.rsqrt(sums[0] / entries + 1e-06)
    fc_step, head_step = scaled(fc_grad, head_grad.reshape(ZH, ZL, width, slab), scale)
    return (fc_step.reshape(fc_weight.shape), head_step, sums[1])


def solution(mesh):
    fine = Mesh(mesh.devices.reshape(X, C, Y, ZH, ZL), ("x", "core", "y", "zh", "zl"))
    tgt, dp, vocab = ("x", "core"), ("y", "zh"), ("zl",)
    in_specs = (
        P(None, dp, tgt),
        P(None, tgt, dp + vocab),
        P(dp + vocab, tgt),
        P(dp, tgt + vocab),
        P(),
        P(),
        P(),
        P(),
    )
    out_specs = (P(None, tgt, dp + vocab), P(dp + vocab, tgt), P())
    return jax.shard_map(
        per_device, mesh=fine, in_specs=in_specs, out_specs=out_specs, check_vma=False
    )
```
